32 devices in a mesh: groups: 2 (over x), rows: 8 (over z, y), wide: 2 (over core).
Axes of the slice: x: 2, y: 2, z: 4, core: 2. Of those that a mesh axis runs over, the one named last changes fastest.
Arguments:
- activations: bfloat16 [8192, 3584], P(('groups', 'rows')), parts along dimension 0
- cotangents: bfloat16 [8192, 2560], P(('groups', 'rows'), 'wide'), parts along dimension 0
- left_root: float32 [7168, 3584], P(('groups', 'rows')), parts along dimension 0, as said below
- right_root: float32 [4, 1280, 1280], P(('groups', 'wide')), parts along dimension 0, as said below
- momentum: float32 [7168, 2560], P(('groups', 'rows'), 'wide'), parts along dimension 0, may hold values from -6 to 6
- second_moment: float32 [7168, 2560], P(('groups', 'rows'), 'wide'), parts along dimension 0, may hold values from 0.25 to 1
Outputs:
- new_momentum: float32 [7168, 2560], P(('groups', 'rows'), 'wide'), parts along dimension 0
- new_second: float32 [7168, 2560], P(('groups', 'rows'), 'wide'), parts along dimension 0
The draws below stay inside these ranges and needn't reach their ends.
There are 2 independent parts, one for each index of `groups`. The reference program is written for one: setup_inputs(seed, part) draws one part's arguments, and reference() takes and returns one part's arrays. A program takes and returns all parts, laid end to end along the dimension named above; each array names one. Nothing has to cross between parts.
Inputs may be any that keep to these rules, and one draw needn't show every extreme that they name: left_root is symmetric positive definite. Each block right_root[w] is symmetric positive definite.
All inputs are finite; a program needn't handle non-finite values.
Results may differ from the reference program's by a relative error of at most 0.01.
Values may be sent and summed in bfloat16 or wider, within the bound.
A program may use at most 192 MiB of HBM per device.

```python
import math
import jax
import jax.numpy as jnp
from jax import lax

LB = 3584
RB = 1280
TOK = 512
TOKENS = 4096
COLS = 2560
N_ROWS = 8
N_WIDE = 2


def draw_activations(key, part):
    key = jax.random.fold_in(key, 11)
    key_noise, key_rough, key_owner = jax.random.split(key, 3)
    column_index = jnp.arange(LB)
    ramp_scale = 10.0 ** (column_index.astype(jnp.float32) / LB - 0.5)
    rough_scale = jax.random.uniform(key_rough, (LB,), jnp.float32, 0.7, 1.4)
    owners = jax.random.permutation(key_owner, N_ROWS)
    replica_index = jnp.arange(TOKENS) // TOK
    target_block = owners[replica_index]
    column_block = column_index // (LB // N_ROWS)
    spike_factor = jnp.where(target_block[:, None] == column_block[None, :], 3.0, 1.0)
    values = jax.random.normal(key_noise, (TOKENS, LB), jnp.float32)
    return (values * (ramp_scale * rough_scale)[None, :] * spike_factor).astype(jnp.bfloat16)


def draw_cotangents(key, part):
    key = jax.random.fold_in(key, 23)
    key_noise, key_rough, key_order = jax.random.split(key, 3)
    column_order = jax.random.permutation(key_order, COLS)
    column_scale = 10.0 ** ((column_order.astype(jnp.float32) + 0.5) / COLS - 0.5)
    rough_scale = jax.random.uniform(key_rough, (COLS,), jnp.float32, 0.7, 1.4)
    values = jax.random.normal(key_noise, (TOKENS, COLS), jnp.float32)
    return (values * (column_scale * rough_scale)[None, :] * (0.5 * TOKENS ** (-0.5))).astype(jnp.bfloat16)


def draw_left_root(key, part):
    key = jax.random.fold_in(key, 37)
    key_noise, key_diagonal = jax.random.split(key, 2)
    noise = jax.random.normal(key_noise, (LB, LB), jnp.float32)
    symmetric = (noise + noise.T) * (0.3 / math.sqrt(2.0 * LB))
    diagonal = jax.random.uniform(key_diagonal, (LB,), jnp.float32, 0.8, 1.2)
    return symmetric + jnp.diag(diagonal)


def draw_right_root(key, part):
    key = jax.random.fold_in(key, 41)
    key_noise, key_diagonal = jax.random.split(key, 2)
    noise = jax.random.normal(key_noise, (N_WIDE, RB, RB), jnp.float32)
    symmetric = (noise + jnp.transpose(noise, (0, 2, 1))) * (0.3 / math.sqrt(2.0 * RB))
    diagonal = jax.random.uniform(key_diagonal, (N_WIDE, RB), jnp.float32, 0.8, 1.2)
    identity = jnp.eye(RB, dtype=jnp.float32)
    return symmetric + diagonal[:, :, None] * identity[None, :, :]


def shard_levels(own_key, dims, cuts, low, largest):
    def one(axis_at, parts):
        draws = jax.random.uniform(jax.random.fold_in(jax.random.fold_in(own_key, 6), axis_at), (parts,), jnp.float32, low / len(cuts), largest / len(cuts))
        return jnp.repeat(jnp.exp(draws), dims[axis_at] // parts).reshape((-1,) + (1,) * (len(dims) - axis_at - 1))

    level = one(*cuts[0])
    for cut in cuts[1:]:
        level = level * one(*cut)
    return level


def bell_draw(key, extent, deviation, reach, cuts=(), held_as=jnp.bfloat16):
    array = deviation * jax.random.normal(key, extent, jnp.float32)
    if cuts:
        array = array * shard_levels(key, extent, cuts, -0.22, 0.18)
    return jnp.clip(array, -reach, reach).astype(held_as)


def setup_inputs(seed: int = 0, part: int = 0) -> dict:
    keys = jax.random.split(jax.random.key(seed), 7)
    part_keys = jax.random.split(jax.random.fold_in(keys[6], part), 7)
    activations = draw_activations(jax.random.fold_in(jax.random.fold_in(keys[6], part), 71), part)
    cotangents = draw_cotangents(jax.random.fold_in(jax.random.fold_in(keys[6], part), 71), part)
    left_root = draw_left_root(jax.random.fold_in(jax.random.fold_in(keys[6], part), 71), part)
    right_root = draw_right_root(jax.random.fold_in(jax.random.fold_in(keys[6], part), 71), part)
    momentum = bell_draw(part_keys[4], (LB, COLS), 1.0, 6.0, ((0, 8), (1, 2)), jnp.float32)
    second_moment = jnp.clip(jnp.exp(math.log(1.0) - 1.3862944 * jax.random.uniform(part_keys[5], (LB, COLS), jnp.float32) ** shard_levels(part_keys[5], (LB, COLS), ((0, 8), (1, 2)), -0.2, 0.2)), 0.25, 1.0)
    return {"activations": activations, "cotangents": cotangents, "left_root": left_root, "right_root": right_root, "momentum": momentum, "second_moment": second_moment}


BETA_ONE = 0.9
BETA_TWO = 0.99
GRAFT_EPS = 1e-08
NORM_EPS = 1e-06

def reference(activations, cotangents, left_root, right_root, momentum, second_moment):

    def add_replica(total, replica):
        first = (replica * TOK).astype(jnp.int32)
        inputs = lax.dynamic_slice_in_dim(activations, first, TOK, 0)
        upstream = lax.dynamic_slice_in_dim(cotangents, first, TOK, 0)
        partial_term = lax.dot_general(inputs, upstream, (((0,), (0,)), ((), ())), preferred_element_type=jnp.float32)
        rounded = lax.optimization_barrier(partial_term.astype(jnp.bfloat16))
        return (total + rounded.astype(jnp.float32), None)
    gradient, _ = lax.scan(add_replica, jnp.zeros((LB, COLS), jnp.float32), jnp.arange(N_ROWS, dtype=jnp.int32))
    new_second = BETA_TWO * second_moment + (1.0 - BETA_TWO) * gradient * gradient
    direction = gradient / (jnp.sqrt(new_second) + GRAFT_EPS)
    rounded_gradient = lax.optimization_barrier(gradient.astype(jnp.bfloat16))
    left_product = jnp.dot(left_root, rounded_gradient.astype(jnp.float32), precision=lax.Precision.HIGHEST, preferred_element_type=jnp.float32)
    left_blocks = left_product.reshape(LB, N_WIDE, RB)
    preconditioned = jnp.einsum('lwr,wrs->lws', left_blocks, right_root, precision=lax.Precision.HIGHEST)
    graft_blocks = direction.reshape(LB, N_WIDE, RB)
    graft_sq = lax.optimization_barrier(jnp.sum(graft_blocks * graft_blocks, axis=(0, 2)))
    root_sq = lax.optimization_barrier(jnp.sum(preconditioned * preconditioned, axis=(0, 2)))
    factor = jnp.sqrt(graft_sq) / jnp.sqrt(root_sq + NORM_EPS)
    new_momentum = BETA_ONE * momentum.reshape(LB, N_WIDE, RB) + factor[None, :, None] * preconditioned
    return (new_momentum.reshape(LB, COLS), new_second)
```

```python
import functools

import jax
import jax.numpy as jnp
from jax import lax
from jax.experimental import pallas as pl
from jax.experimental.pallas import tpu as pltpu
from jax.sharding import PartitionSpec as P

BETA_ONE = 0.9
BETA_TWO = 0.99
GRAFT_EPS = 1e-08
NORM_EPS = 1e-06
CW = 256
MESH = pl.DeviceIdType.MESH
F32 = jnp.float32
BF16 = jnp.bfloat16


def kernel(
    n, wides, m, nc, blk, tok,
    at_in, c_in, l2, r_in, second,
    pre, g_out, tot,
    at2, cc, rbuf, lbuf, gbuf, lown, lr, pps, ppr, rv, sv, d2,
    loc, locc, xa_s, xa_r, xc_s, xc_r, xl_s, xl_r,
    rr_s, rr_r, rl_s, rl_r, ga_r, gr_s, gl_s, pp_s, pp_r, st_s, st_r,
):
    me = lax.axis_index("rows")
    w = lax.axis_index("wide")
    k = me // 2
    p = me % 2
    other = 1 - w
    partner = k * 2 + (1 - p)
    right = jnp.minimum(k + 1, m - 1) * 2 + p
    left = jnp.maximum(k - 1, 0) * 2 + p
    mh = m // wides

    def remote(src, dst, ss, rs, **to):
        return pltpu.make_async_remote_copy(
            src_ref=src, dst_ref=dst, send_sem=ss, recv_sem=rs,
            device_id=to, device_id_type=MESH,
        )

    own_at = pltpu.make_async_copy(at_in.at[:, p], at2.at[:, :, pl.ds(0, tok)], loc.at[0])
    own_l = pltpu.make_async_copy(l2.at[p], lown, loc.at[1])
    own_r = pltpu.make_async_copy(r_in, rv, loc.at[2])

    def own_c(c):
        cols = pl.ds(pl.multiple_of(c * CW, CW), CW)
        return pltpu.make_async_copy(c_in.at[:, cols], cc.at[c, pl.ds(0, tok)], locc.at[c])

    half = pl.ds(w * mh, mh)
    ohalf = pl.ds(other * mh, mh)
    part = pl.ds(tok, tok)
    send_at = remote(
        at_in.at[half, 1 - p], at2.at[half, :, part], xa_s.at[0], xa_r.at[0], rows=partner)
    fwd_at = remote(
        at2.at[half, :, part], at2.at[half, :, part], xa_s.at[1], xa_r.at[1], wide=other)
    got_at = remote(
        at2.at[ohalf, :, part], at2.at[ohalf, :, part], xa_s.at[1], xa_r.at[1], wide=other)
    send_l = remote(l2.at[1 - p, w], lr.at[w], xl_s.at[0], xl_r.at[0], rows=partner)
    fwd_l = remote(lr.at[w], lr.at[w], xl_s.at[1], xl_r.at[1], wide=other)
    got_l = remote(lr.at[other], lr.at[other], xl_s.at[1], xl_r.at[1], wide=other)

    def send_c(c):
        cols = pl.ds(pl.multiple_of(c * CW, CW), CW)
        return remote(
            c_in.at[:, cols], cc.at[c, part], xc_s.at[c], xc_r.at[c], rows=partner)

    def rs_right(c, b):
        return remote(
            rbuf.at[c, b], rbuf.at[c, b], rr_s.at[c, b], rr_r.at[c, b], rows=right)

    def rs_left(c, b):
        return remote(lbuf.at[c, b], lbuf.at[c, b], rl_s.at[c, b], rl_r.at[c, b], rows=left)

    def block_rows(b):
        return pl.ds(pl.multiple_of(b * blk, blk), blk)

    def ag_right(c, b):
        ref = gbuf.at[c, block_rows(b)]
        return remote(ref, ref, gr_s.at[c, b], ga_r.at[c, b], rows=right)

    def ag_left(c, b):
        ref = gbuf.at[c, block_rows(b)]
        return remote(ref, ref, gl_s.at[c, b], ga_r.at[c, b], rows=left)

    def send_pp(c):
        return remote(pps.at[c], ppr.at[c], pp_s.at[c], pp_r.at[c], rows=partner)

    barrier = pltpu.get_barrier_semaphore()

    def greet(i, _):
        pl.semaphore_signal(
            barrier, inc=1, device_id={"rows": lax.rem(me + i, n)}, device_id_type=MESH)
        return 0

    own_at.start()
    lax.fori_loop(0, nc, lambda c, _: (own_c(c).start(), 0)[1], 0)
    lax.fori_loop(1, n, greet, 0)
    pl.semaphore_signal(barrier, inc=1, device_id={"wide": other}, device_id_type=MESH)
    pl.semaphore_wait(barrier, n)

    send_c(0).start()
    send_at.start()
    send_c(1).start()
    own_l.start()
    own_r.start()

    @pl.when(k == 0)
    def _():
        rbuf[...] = jnp.zeros_like(rbuf)

    @pl.when(k == m - 1)
    def _():
        lbuf[...] = jnp.zeros_like(lbuf)

    d2[...] = jnp.zeros_like(d2)
    pre[...] = jnp.zeros_like(pre)
    lax.fori_loop(0, nc, lambda c, _: (own_c(c).wait(), 0)[1], 0)
    own_at.wait()
    send_at.wait_recv()
    fwd_at.start()
    got_at.wait_recv()

    def term(c, b):
        return jnp.dot(at2[b], cc[c], preferred_element_type=F32)

    def reduce_step(c):
        @pl.when(c + 2 < nc)
        def _():
            send_c(c + 2).start()

        @pl.when(c == 0)
        def _():
            send_l.start()

        send_c(c).wait_recv()

        def far(i, _):
            d = m - 1 - i

            @pl.when(k + d < m)
            def _():
                b = k + d
                x = term(c, b)

                @pl.when(k > 0)
                def _():
                    rs_right(c, b).wait_recv()

                rbuf[c, b] = (x + rbuf[c, b].astype(F32)).astype(BF16)
                rs_right(c, b).start()

            @pl.when(k - d >= 0)
            def _():
                b = k - d
                x = term(c, b)

                @pl.when(k < m - 1)
                def _():
                    rs_left(c, b).wait_recv()

                lbuf[c, b] = (x + lbuf[c, b].astype(F32)).astype(BF16)
                rs_left(c, b).start()

            return 0

        lax.fori_loop(0, m - 1, far, 0)

    def own_step(c):
        x = term(c, k)

        @pl.when(k > 0)
        def _():
            rs_right(c, k).wait_recv()

        @pl.when(k < m - 1)
        def _():
            rs_left(c, k).wait_recv()

        g = x + rbuf[c, k].astype(F32) + lbuf[c, k].astype(F32)
        gbuf[c, block_rows(k)] = g.astype(BF16)

        @pl.when(k < m - 1)
        def _():
            ag_right(c, k).start()

        @pl.when(k > 0)
        def _():
            ag_left(c, k).start()

        cols = pl.ds(pl.multiple_of(c * CW, CW), CW)
        g_out[:, cols] = g
        new = BETA_TWO * second[:, cols] + (1.0 - BETA_TWO) * g * g
        direction = g / (jnp.sqrt(new) + GRAFT_EPS)
        d2[...] += jnp.sum((direction * direction).reshape(blk // 8, 8, CW), axis=0)

    def gather_step(c):
        def near(d, _):
            @pl.when(k - d >= 0)
            def _():
                ag_right(c, k - d).wait_recv()

                @pl.when(k < m - 1)
                def _():
                    ag_right(c, k - d).start()

            @pl.when(k + d < m)
            def _():
                ag_left(c, k + d).wait_recv()

                @pl.when(k > 0)
                def _():
                    ag_left(c, k + d).start()

            return 0

        lax.fori_loop(1, m, near, 0)

    def times(lref, c):
        kh = (m * blk) // wides
        x = jnp.dot(lref[0], gbuf[c, pl.ds(0, kh)], preferred_element_type=F32)
        for h in range(1, wides):
            x += jnp.dot(lref[h], gbuf[c, pl.ds(h * kh, kh)], preferred_element_type=F32)
        return x

    def left_step(c):
        @pl.when(c == 0)
        def _():
            own_l.wait()
            got_l.wait_recv()

        pps[c] = times(lr, c).astype(BF16)
        send_pp(c).start()

    def right_step(c):
        @pl.when(c == 0)
        def _():
            own_r.wait()

        x = times(lown, c)
        send_pp(c).wait_recv()
        x = (x + ppr[c].astype(F32)).astype(BF16)
        depth = pl.ds(pl.multiple_of(c * CW, CW), CW)

        def tile(j, _):
            cols = pl.ds(pl.multiple_of(j * CW, CW), CW)
            pre[:, cols] += jnp.dot(
                x, rv[depth, cols].astype(BF16), preferred_element_type=F32)
            return 0

        lax.fori_loop(0, nc, tile, 0)

    def step(t, _):
        @pl.when(t < nc)
        def _():
            reduce_step(t)

        @pl.when((t >= 1) & (t < nc + 1))
        def _():
            own_step(t - 1)

        @pl.when(t == 1)
        def _():
            send_l.wait_recv()
            fwd_l.start()

        @pl.when((t >= 2) & (t < nc + 2))
        def _():
            gather_step(t - 2)
            left_step(t - 2)

        @pl.when((t >= 3) & (t < nc + 3))
        def _():
            right_step(t - 3)

        return 0

    lax.fori_loop(0, nc + 3, step, 0)

    graft = jnp.sum(d2[...])
    x = pre[...]
    root = jnp.sum(x * x)
    rows8 = lax.broadcasted_iota(jnp.int32, (8, 128), 0)
    sv[me] = jnp.where(rows8 == 0, graft, root)

    def stat(peer, src):
        return remote(sv.at[src], sv.at[src], st_s.at[peer], st_r.at[src], rows=peer)

    def peer_of(i):
        return lax.rem(me + i, n)

    lax.fori_loop(1, n, lambda i, _: (stat(peer_of(i), me).start(), 0)[1], 0)

    def drain(c, _):
        send_c(c).wait_send()
        send_pp(c).wait_send()

        def each(b, _):
            @pl.when(b > k)
            def _():
                rs_right(c, b).wait_send()

            @pl.when(b < k)
            def _():
                rs_left(c, b).wait_send()

            @pl.when((b <= k) & (k < m - 1))
            def _():
                ag_right(c, b).wait_send()

            @pl.when((b >= k) & (k > 0))
            def _():
                ag_left(c, b).wait_send()

            return 0

        lax.fori_loop(0, m, each, 0)
        return 0

    lax.fori_loop(0, nc, drain, 0)
    send_at.wait_send()
    fwd_at.wait_send()
    send_l.wait_send()
    fwd_l.wait_send()
    lax.fori_loop(1, n, lambda i, _: (stat(peer_of(i), peer_of(i)).wait_recv(), 0)[1], 0)
    lax.fori_loop(1, n, lambda i, _: (stat(peer_of(i), me).wait_send(), 0)[1], 0)
    tot[...] = jnp.sum(sv[...], axis=0)


def per_device(n, wides, activations, cotangents, left_root, right_root, momentum, second_moment):
    tok, lb = activations.shape
    rb = cotangents.shape[1]
    blk = left_root.shape[0]
    m = n // 2
    nc = rb // CW
    kh = (m * blk) // wides
    at_in = activations.T.reshape(m, 2, blk, tok)
    l2 = (
        left_root.astype(BF16).reshape(blk, m, 2, blk).transpose(2, 0, 1, 3)
        .reshape(2, blk, wides, kh).transpose(0, 2, 1, 3)
    )
    anywhere = pl.BlockSpec(memory_space=pl.ANY)
    vmem = pl.BlockSpec(memory_space=pltpu.VMEM)
    dma = pltpu.SemaphoreType.DMA
    pre, gradient, tot = pl.pallas_call(
        functools.partial(kernel, n, wides, m, nc, blk, tok),
        out_shape=(
            jax.ShapeDtypeStruct((blk, rb), F32),
            jax.ShapeDtypeStruct((blk, rb), F32),
            jax.ShapeDtypeStruct((8, 128), F32),
        ),
        in_specs=[anywhere, anywhere, anywhere, anywhere, vmem],
        out_specs=(vmem, vmem, vmem),
        scratch_shapes=[
            pltpu.VMEM((m, blk, 2 * tok), BF16),
            pltpu.VMEM((nc, 2 * tok, CW), BF16),
            pltpu.VMEM((nc, m, blk, CW), BF16),
            pltpu.VMEM((nc, m, blk, CW), BF16),
            pltpu.VMEM((nc, m * blk, CW), BF16),
            pltpu.VMEM((wides, blk, kh), BF16),
            pltpu.VMEM((wides, blk, kh), BF16),
            pltpu.VMEM((nc, blk, CW), BF16),
            pltpu.VMEM((nc, blk, CW), BF16),
            pltpu.VMEM((rb, rb), F32),
            pltpu.VMEM((n, 8, 128), F32),
            pltpu.VMEM((8, CW), F32),
            dma((3,)), dma((nc,)), dma((2,)), dma((2,)), dma((nc,)), dma((nc,)),
            dma((2,)), dma((2,)),
            dma((nc, m)), dma((nc, m)), dma((nc, m)), dma((nc, m)),
            dma((nc, m)), dma((nc, m)), dma((nc, m)),
            dma((nc,)), dma((nc,)), dma((n,)), dma((n,)),
        ],
        compiler_params=pltpu.CompilerParams(
            collective_id=0, has_side_effects=True, vmem_limit_bytes=58 * 2**20,
        ),
    )(at_in, cotangents, l2, right_root[0], second_moment)
    new_second = BETA_TWO * second_moment + (1.0 - BETA_TWO) * gradient * gradient
    factor = jnp.sqrt(tot[0, 0]) / jnp.sqrt(tot[1, 0] + NORM_EPS)
    new_momentum = BETA_ONE * momentum + factor * pre
    return (new_momentum, new_second)


def solution(mesh):
    placed = (
        P(("groups", "rows"), None),
        P(("groups", "rows"), "wide"),
        P(("groups", "rows"), None),
        P(("groups", "wide"), None, None),
        P(("groups", "rows"), "wide"),
        P(("groups", "rows"), "wide"),
    )
    return jax.shard_map(
        functools.partial(per_device, mesh.shape["rows"], mesh.shape["wide"]),
        mesh=mesh,
        in_specs=placed,
        out_specs=(P(("groups", "rows"), "wide"), P(("groups", "rows"), "wide")),
        check_vma=False,
    )
```

```python
import functools
import math

import jax
import jax.numpy as jnp
from jax import lax
from jax.experimental import pallas as pl
from jax.experimental.pallas import tpu as pltpu
from jax.sharding import PartitionSpec as P

BETA_ONE = 0.9
BETA_TWO = 0.99
GRAFT_EPS = 1e-08
NORM_EPS = 1e-06
CW = 128
MESH = pl.DeviceIdType.MESH
F32 = jnp.float32
BF16 = jnp.bfloat16


def kernel(
    n, wides, m, nc, blk, tok, win,
    at_in, c_in, l_in, r_in, second,
    pre, g_out, tot,
    at2, cc, rbuf, lbuf, gbuf, lf, lown, ls, lr, pps, ppr, rv, sv, d2,
    loc, locc, xa_s, xa_r, xc_s, xc_r, xl_s, xl_r,
    rr_s, rr_r, rl_s, rl_r, ga_r, gr_s, gl_s, pp_s, pp_r, st_s, st_r,
):
    me = lax.axis_index("rows")
    w = lax.axis_index("wide")
    k = me // 2
    p = me % 2
    other = 1 - w
    partner = k * 2 + (1 - p)
    right = jnp.minimum(k + 1, m - 1) * 2 + p
    left = jnp.maximum(k - 1, 0) * 2 + p
    mh = m // wides

    def remote(src, dst, ss, rs, **to):
        return pltpu.make_async_remote_copy(
            src_ref=src, dst_ref=dst, send_sem=ss, recv_sem=rs,
            device_id=to, device_id_type=MESH,
        )

    own_at = pltpu.make_async_copy(at_in.at[:, p], at2.at[:, :, pl.ds(0, tok)], loc.at[0])
    own_l = pltpu.make_async_copy(l_in, lf, loc.at[1])
    own_r = pltpu.make_async_copy(r_in, rv, loc.at[2])

    def own_c(c):
        cols = pl.ds(pl.multiple_of(c * CW, CW), CW)
        return pltpu.make_async_copy(c_in.at[:, cols], cc.at[c, pl.ds(0, tok)], locc.at[c])

    half = pl.ds(w * mh, mh)
    ohalf = pl.ds(other * mh, mh)
    part = pl.ds(tok, tok)
    tw = tok // wides
    part_w = pl.ds(pl.multiple_of(tok + w * tw, tw), tw)
    part_o = pl.ds(pl.multiple_of(tok + other * tw, tw), tw)
    token_w = pl.ds(pl.multiple_of(w * tw, tw), tw)

    def send_at(b):
        return remote(
            at_in.at[b, 1 - p, :, token_w], at2.at[b, :, part_w], xa_s.at[0, b], xa_r.at[0, b],
            rows=partner)

    def fwd_at(b):
        return remote(
            at2.at[b, :, part_w], at2.at[b, :, part_w], xa_s.at[1, b], xa_r.at[1, b], wide=other)

    def got_at(b):
        return remote(
            at2.at[b, :, part_o], at2.at[b, :, part_o], xa_s.at[1, b], xa_r.at[1, b], wide=other)

    def far_first(f):
        def both(i, _):
            d = m - 1 - i

            @pl.when(k + d < m)
            def _():
                f(k + d)

            @pl.when(k - d >= 0)
            def _():
                f(k - d)

            return 0

        lax.fori_loop(0, m - 1, both, 0)
        f(k)

    def window(b, q):
        first = (2 * b + q) * blk
        start = jnp.minimum(first // 128 * 128, n * blk - win)
        return pl.multiple_of(start, 128), first - start

    send_l = remote(ls.at[half], lr.at[half], xl_s.at[0], xl_r.at[0], rows=partner)
    fwd_l = remote(lr.at[half], lr.at[half], xl_s.at[1], xl_r.at[1], wide=other)
    got_l = remote(lr.at[ohalf], lr.at[ohalf], xl_s.at[1], xl_r.at[1], wide=other)

    def send_c(c):
        cols = pl.ds(pl.multiple_of(c * CW, CW), CW)
        return remote(
            c_in.at[:, cols], cc.at[c, part], xc_s.at[c], xc_r.at[c], rows=partner)

    def rs_right(c, b):
        return remote(
            rbuf.at[c, b], rbuf.at[c, b], rr_s.at[c, b], rr_r.at[c, b], rows=right)

    def rs_left(c, b):
        return remote(lbuf.at[c, b], lbuf.at[c, b], rl_s.at[c, b], rl_r.at[c, b], rows=left)

    def block_rows(b):
        return pl.ds(pl.multiple_of(b * win + window(b, p)[1], 16), blk)

    def ag_right(c, b):
        ref = gbuf.at[c, block_rows(b)]
        return remote(ref, ref, gr_s.at[c, b], ga_r.at[c, b], rows=right)

    def ag_left(c, b):
        ref = gbuf.at[c, block_rows(b)]
        return remote(ref, ref, gl_s.at[c, b], ga_r.at[c, b], rows=left)

    def send_pp(c):
        return remote(pps.at[c], ppr.at[c], pp_s.at[c], pp_r.at[c], rows=partner)

    barrier = pltpu.get_barrier_semaphore()

    def greet(i, _):
        pl.semaphore_signal(
            barrier, inc=1, device_id={"rows": lax.rem(me + i, n)}, device_id_type=MESH)
        return 0

    own_at.start()
    lax.fori_loop(0, nc, lambda c, _: (own_c(c).start(), 0)[1], 0)
    lax.fori_loop(1, n, greet, 0)
    pl.semaphore_signal(barrier, inc=1, device_id={"wide": other}, device_id_type=MESH)
    gbuf[...] = jnp.zeros_like(gbuf)

    @pl.when(k == 0)
    def _():
        rbuf[...] = jnp.zeros_like(rbuf)

    @pl.when(k == m - 1)
    def _():
        lbuf[...] = jnp.zeros_like(lbuf)

    pl.semaphore_wait(barrier, n)

    send_c(0).start()
    far_first(lambda b: send_at(b).start())
    send_c(1).start()
    own_l.start()
    own_r.start()
    d2[...] = jnp.zeros_like(d2)
    pre[...] = jnp.zeros_like(pre)
    own_at.wait()

    def arrive(c, b):
        @pl.when(c == 0)
        def _():
            send_at(b).wait_recv()
            fwd_at(b).start()
            got_at(b).wait_recv()

    def cast_left():
        own_l.wait()

        def one(b, _):
            mine, _ = window(b, p)
            theirs, _ = window(b, 1 - p)
            ls[b] = lf[:, pl.ds(theirs, win)].astype(BF16)
            lown[b] = lf[:, pl.ds(mine, win)].astype(BF16)
            return 0

        lax.fori_loop(0, m, one, 0)

    def term(c, b):
        return jnp.dot(at2[b], cc[c], preferred_element_type=F32)

    def reduce_step(c):
        @pl.when(c + 2 < nc)
        def _():
            send_c(c + 2).start()

        own_c(c).wait()
        send_c(c).wait_recv()

        def far(i, _):
            d = m - 1 - i

            @pl.when(k + d < m)
            def _():
                b = k + d
                arrive(c, b)
                x = term(c, b)

                @pl.when(k > 0)
                def _():
                    rs_right(c, b).wait_recv()

                rbuf[c, b] = (x + rbuf[c, b].astype(F32)).astype(BF16)
                rs_right(c, b).start()

            @pl.when(k - d >= 0)
            def _():
                b = k - d
                arrive(c, b)
                x = term(c, b)

                @pl.when(k < m - 1)
                def _():
                    rs_left(c, b).wait_recv()

                lbuf[c, b] = (x + lbuf[c, b].astype(F32)).astype(BF16)
                rs_left(c, b).start()

            return 0

        lax.fori_loop(0, m - 1, far, 0)
        arrive(c, k)

        @pl.when(c == 0)
        def _():
            cast_left()
            send_l.start()

    def own_step(c):
        x = term(c, k)

        @pl.when(k > 0)
        def _():
            rs_right(c, k).wait_recv()

        @pl.when(k < m - 1)
        def _():
            rs_left(c, k).wait_recv()

        g = x + rbuf[c, k].astype(F32) + lbuf[c, k].astype(F32)
        gbuf[c, block_rows(k)] = g.astype(BF16)

        @pl.when(k < m - 1)
        def _():
            ag_right(c, k).start()

        @pl.when(k > 0)
        def _():
            ag_left(c, k).start()

        cols = pl.ds(pl.multiple_of(c * CW, CW), CW)
        g_out[:, cols] = g
        new = BETA_TWO * second[:, cols] + (1.0 - BETA_TWO) * g * g
        direction = g / (jnp.sqrt(new) + GRAFT_EPS)
        d2[...] += jnp.sum((direction * direction).reshape(blk // 8, 8, CW), axis=0)

    def gather_step(c):
        def near(d, _):
            @pl.when(k - d >= 0)
            def _():
                ag_right(c, k - d).wait_recv()

                @pl.when(k < m - 1)
                def _():
                    ag_right(c, k - d).start()

            @pl.when(k + d < m)
            def _():
                ag_left(c, k + d).wait_recv()

                @pl.when(k > 0)
                def _():
                    ag_left(c, k + d).start()

            return 0

        lax.fori_loop(1, m, near, 0)

    def times(lref, c):
        x = jnp.dot(lref[0], gbuf[c, pl.ds(0, win)], preferred_element_type=F32)
        for b in range(1, m):
            x += jnp.dot(lref[b], gbuf[c, pl.ds(b * win, win)], preferred_element_type=F32)
        return x

    def left_step(c):
        @pl.when(c == 0)
        def _():
            got_l.wait_recv()

        pps[c] = times(lr, c).astype(BF16)
        send_pp(c).start()

    def right_step(c):
        @pl.when(c == 0)
        def _():
            own_r.wait()

        x = times(lown, c)
        send_pp(c).wait_recv()
        x = (x + ppr[c].astype(F32)).astype(BF16)
        depth = pl.ds(pl.multiple_of(c * CW, CW), CW)

        def tile(j, _):
            cols = pl.ds(pl.multiple_of(j * 256, 256), 256)
            pre[:, cols] += jnp.dot(
                x, rv[depth, cols].astype(BF16), preferred_element_type=F32)
            return 0

        lax.fori_loop(0, pre.shape[1] // 256, tile, 0)

    def step(t, _):
        @pl.when(t < nc)
        def _():
            reduce_step(t)

        @pl.when((t >= 1) & (t < nc + 1))
        def _():
            own_step(t - 1)

        @pl.when(t == 1)
        def _():
            send_l.wait_recv()
            fwd_l.start()

        @pl.when((t >= 2) & (t < nc + 2))
        def _():
            gather_step(t - 2)
            left_step(t - 2)

        @pl.when((t >= 3) & (t < nc + 3))
        def _():
            right_step(t - 3)

        return 0

    lax.fori_loop(0, nc + 3, step, 0)

    graft = jnp.sum(d2[...])
    x = pre[...]
    root = jnp.sum(x * x)
    rows8 = lax.broadcasted_iota(jnp.int32, (8, 128), 0)
    sv[me] = jnp.where(rows8 == 0, graft, root)

    def stat(peer, src):
        return remote(sv.at[src], sv.at[src], st_s.at[peer], st_r.at[src], rows=peer)

    def peer_of(i):
        return lax.rem(me + i, n)

    lax.fori_loop(1, n, lambda i, _: (stat(peer_of(i), me).start(), 0)[1], 0)

    def drain(c, _):
        send_c(c).wait_send()
        send_pp(c).wait_send()

        def each(b, _):
            @pl.when(c == 0)
            def _():
                send_at(b).wait_send()
                fwd_at(b).wait_send()

            @pl.when(b > k)
            def _():
                rs_right(c, b).wait_send()

            @pl.when(b < k)
            def _():
                rs_left(c, b).wait_send()

            @pl.when((b <= k) & (k < m - 1))
            def _():
                ag_right(c, b).wait_send()

            @pl.when((b >= k) & (k > 0))
            def _():
                ag_left(c, b).wait_send()

            return 0

        lax.fori_loop(0, m, each, 0)
        return 0

    lax.fori_loop(0, nc, drain, 0)
    send_l.wait_send()
    fwd_l.wait_send()
    lax.fori_loop(1, n, lambda i, _: (stat(peer_of(i), peer_of(i)).wait_recv(), 0)[1], 0)
    lax.fori_loop(1, n, lambda i, _: (stat(peer_of(i), me).wait_send(), 0)[1], 0)
    tot[...] = jnp.sum(sv[...], axis=0)


def per_device(n, wides, activations, cotangents, left_root, right_root, momentum, second_moment):
    tok, lb = activations.shape
    rb = cotangents.shape[1]
    blk = left_root.shape[0]
    m = n // 2
    nc = rb // CW
    win = -(-(blk + 128 - math.gcd(blk, 128)) // 128) * 128
    at_in = activations.T.reshape(m, 2, blk, tok)
    anywhere = pl.BlockSpec(memory_space=pl.ANY)
    vmem = pl.BlockSpec(memory_space=pltpu.VMEM)
    dma = pltpu.SemaphoreType.DMA
    pre, gradient, tot = pl.pallas_call(
        functools.partial(kernel, n, wides, m, nc, blk, tok, win),
        out_shape=(
            jax.ShapeDtypeStruct((blk, rb), F32),
            jax.ShapeDtypeStruct((blk, rb), F32),
            jax.ShapeDtypeStruct((8, 128), F32),
        ),
        in_specs=[anywhere, anywhere, anywhere, anywhere, vmem],
        out_specs=(vmem, vmem, vmem),
        scratch_shapes=[
            pltpu.VMEM((m, blk, 2 * tok), BF16),
            pltpu.VMEM((nc, 2 * tok, CW), BF16),
            pltpu.VMEM((nc, m, blk, CW), BF16),
            pltpu.VMEM((nc, m, blk, CW), BF16),
            pltpu.VMEM((nc, m * win, CW), BF16),
            pltpu.VMEM((blk, n * blk), F32),
            pltpu.VMEM((m, blk, win), BF16),
            pltpu.VMEM((m, blk, win), BF16),
            pltpu.VMEM((m, blk, win), BF16),
            pltpu.VMEM((nc, blk, CW), BF16),
            pltpu.VMEM((nc, blk, CW), BF16),
            pltpu.VMEM((rb, rb), F32),
            pltpu.VMEM((n, 8, 128), F32),
            pltpu.VMEM((8, CW), F32),
            dma((3,)), dma((nc,)), dma((2, m)), dma((2, m)), dma((nc,)), dma((nc,)),
            dma((2,)), dma((2,)),
            dma((nc, m)), dma((nc, m)), dma((nc, m)), dma((nc, m)),
            dma((nc, m)), dma((nc, m)), dma((nc, m)),
            dma((nc,)), dma((nc,)), dma((n,)), dma((n,)),
        ],
        compiler_params=pltpu.CompilerParams(
            collective_id=0, has_side_effects=True, vmem_limit_bytes=58 * 2**20,
        ),
    )(at_in, cotangents, left_root, right_root[0], second_moment)
    new_second = BETA_TWO * second_moment + (1.0 - BETA_TWO) * gradient * gradient
    factor = jnp.sqrt(tot[0, 0]) / jnp.sqrt(tot[1, 0] + NORM_EPS)
    new_momentum = BETA_ONE * momentum + factor * pre
    return (new_momentum, new_second)


def solution(mesh):
    placed = (
        P(("groups", "rows"), None),
        P(("groups", "rows"), "wide"),
        P(("groups", "rows"), None),
        P(("groups", "wide"), None, None),
        P(("groups", "rows"), "wide"),
        P(("groups", "rows"), "wide"),
    )
    return jax.shard_map(
        functools.partial(per_device, mesh.shape["rows"], mesh.shape["wide"]),
        mesh=mesh,
        in_specs=placed,
        out_specs=(P(("groups", "rows"), "wide"), P(("groups", "rows"), "wide")),
        check_vma=False,
    )
```

```python
import functools
import math

import jax
import jax.numpy as jnp
from jax import lax
from jax.experimental import pallas as pl
from jax.experimental.pallas import tpu as pltpu
from jax.sharding import PartitionSpec as P

BETA_ONE = 0.9
BETA_TWO = 0.99
GRAFT_EPS = 1e-08
NORM_EPS = 1e-06
CW = 128
MESH = pl.DeviceIdType.MESH
F32 = jnp.float32
BF16 = jnp.bfloat16


def kernel(
    n, wides, m, nc, blk, tok, win,
    at_in, c_in, l_in, r_in, second,
    pre, g_out, tot,
    at2, cc, rbuf, lbuf, gbuf, lf, lown, ls, lr, pps, ppr, rv, sv, d2,
    loc, locc, xa_s, xa_r, xc_s, xc_r, xl_s, xl_r,
    rr_s, rr_r, rl_s, rl_r, ga_r, gr_s, gl_s, pp_s, pp_r, st_s, st_r,
):
    me = lax.axis_index("rows")
    w = lax.axis_index("wide")
    k = me // 2
    p = me % 2
    other = 1 - w
    partner = k * 2 + (1 - p)
    right = jnp.minimum(k + 1, m - 1) * 2 + p
    left = jnp.maximum(k - 1, 0) * 2 + p
    mh = m // wides

    def remote(src, dst, ss, rs, **to):
        return pltpu.make_async_remote_copy(
            src_ref=src, dst_ref=dst, send_sem=ss, recv_sem=rs,
            device_id=to, device_id_type=MESH,
        )

    own_at = pltpu.make_async_copy(at_in.at[:, p], at2.at[:, :, pl.ds(0, tok)], loc.at[0])
    own_l = pltpu.make_async_copy(l_in, lf, loc.at[1])
    own_r = pltpu.make_async_copy(r_in, rv, loc.at[2])

    def own_c(c):
        cols = pl.ds(pl.multiple_of(c * CW, CW), CW)
        return pltpu.make_async_copy(c_in.at[:, cols], cc.at[c, pl.ds(0, tok)], locc.at[c])

    half = pl.ds(w * mh, mh)
    ohalf = pl.ds(other * mh, mh)
    part = pl.ds(tok, tok)
    tw = tok // wides
    part_w = pl.ds(pl.multiple_of(tok + w * tw, tw), tw)
    part_o = pl.ds(pl.multiple_of(tok + other * tw, tw), tw)
    token_w = pl.ds(pl.multiple_of(w * tw, tw), tw)

    def send_at(b):
        return remote(
            at_in.at[b, 1 - p, :, token_w], at2.at[b, :, part_w], xa_s.at[0, b], xa_r.at[0, b],
            rows=partner)

    def fwd_at(b):
        return remote(
            at2.at[b, :, part_w], at2.at[b, :, part_w], xa_s.at[1, b], xa_r.at[1, b], wide=other)

    def got_at(b):
        return remote(
            at2.at[b, :, part_o], at2.at[b, :, part_o], xa_s.at[1, b], xa_r.at[1, b], wide=other)

    def far_first(f):
        def both(i, _):
            d = m - 1 - i

            @pl.when(k + d < m)
            def _():
                f(k + d)

            @pl.when(k - d >= 0)
            def _():
                f(k - d)

            return 0

        lax.fori_loop(0, m - 1, both, 0)
        f(k)

    def window(b, q):
        first = (2 * b + q) * blk
        start = jnp.minimum(first // 128 * 128, n * blk - win)
        return pl.multiple_of(start, 128), first - start

    send_l = remote(ls.at[half], lr.at[half], xl_s.at[0], xl_r.at[0], rows=partner)
    fwd_l = remote(lr.at[half], lr.at[half], xl_s.at[1], xl_r.at[1], wide=other)
    got_l = remote(lr.at[ohalf], lr.at[ohalf], xl_s.at[1], xl_r.at[1], wide=other)

    def send_c(c):
        cols = pl.ds(pl.multiple_of(c * CW, CW), CW)
        return remote(
            c_in.at[:, cols], cc.at[c, part], xc_s.at[c], xc_r.at[c], rows=partner)

    def rs_right(c, b):
        return remote(
            rbuf.at[c, b], rbuf.at[c, b], rr_s.at[c, b], rr_r.at[c, b], rows=right)

    def rs_left(c, b):
        return remote(lbuf.at[c, b], lbuf.at[c, b], rl_s.at[c, b], rl_r.at[c, b], rows=left)

    def block_rows(b):
        return pl.ds(pl.multiple_of(b * win + window(b, p)[1], 16), blk)

    def ag_right(c, b):
        ref = gbuf.at[c, block_rows(b)]
        return remote(ref, ref, gr_s.at[c, b], ga_r.at[c, b], rows=right)

    def ag_left(c, b):
        ref = gbuf.at[c, block_rows(b)]
        return remote(ref, ref, gl_s.at[c, b], ga_r.at[c, b], rows=left)

    def send_pp(c):
        return remote(pps.at[c], ppr.at[c], pp_s.at[c], pp_r.at[c], rows=partner)

    barrier = pltpu.get_barrier_semaphore()

    def greet(i, _):
        pl.semaphore_signal(
            barrier, inc=1, device_id={"rows": lax.rem(me + i, n)}, device_id_type=MESH)
        return 0

    own_at.start()
    lax.fori_loop(0, nc, lambda c, _: (own_c(c).start(), 0)[1], 0)
    lax.fori_loop(1, n, greet, 0)
    pl.semaphore_signal(barrier, inc=1, device_id={"wide": other}, device_id_type=MESH)
    gbuf[...] = jnp.zeros_like(gbuf)

    @pl.when(k == 0)
    def _():
        rbuf[...] = jnp.zeros_like(rbuf)

    @pl.when(k == m - 1)
    def _():
        lbuf[...] = jnp.zeros_like(lbuf)

    pl.semaphore_wait(barrier, n)

    send_c(0).start()
    far_first(lambda b: send_at(b).start())
    send_c(1).start()
    own_l.start()
    own_r.start()
    d2[...] = jnp.zeros_like(d2)
    pre[...] = jnp.zeros_like(pre)
    own_at.wait()

    def arrive(c, b):
        @pl.when(c == 0)
        def _():
            send_at(b).wait_recv()
            fwd_at(b).start()
            got_at(b).wait_recv()

    def cast_left():
        own_l.wait()

        def one(b, _):
            mine, _ = window(b, p)
            theirs, _ = window(b, 1 - p)
            ls[b] = lf[:, pl.ds(theirs, win)].astype(BF16)
            lown[b] = lf[:, pl.ds(mine, win)].astype(BF16)
            return 0

        lax.fori_loop(0, m, one, 0)

    def term(c, b):
        return jnp.dot(at2[b], cc[c], preferred_element_type=F32)

    def chunk_step(c):
        @pl.when(c + 2 < nc)
        def _():
            send_c(c + 2).start()

        own_c(c).wait()
        send_c(c).wait_recv()

    def right_pass(c):
        def one(i, _):
            b = m - 1 - i
            arrive(c, b)
            x = term(c, b)

            @pl.when(k > 0)
            def _():
                rs_right(c, b).wait_recv()

            rbuf[c, b] = (x + rbuf[c, b].astype(F32)).astype(BF16)
            rs_right(c, b).start()
            return 0

        lax.fori_loop(0, m - 1 - k, one, 0)

    def left_pass(c):
        def one(b, _):
            arrive(c, b)
            x = term(c, b)

            @pl.when(k < m - 1)
            def _():
                rs_left(c, b).wait_recv()

            lbuf[c, b] = (x + lbuf[c, b].astype(F32)).astype(BF16)
            rs_left(c, b).start()
            return 0

        lax.fori_loop(0, k, one, 0)

    def own_step(c):
        arrive(c, k)
        x = term(c, k)

        @pl.when(k > 0)
        def _():
            rs_right(c, k).wait_recv()

        @pl.when(k < m - 1)
        def _():
            rs_left(c, k).wait_recv()

        g = x + rbuf[c, k].astype(F32) + lbuf[c, k].astype(F32)
        gbuf[c, block_rows(k)] = g.astype(BF16)

        @pl.when(k < m - 1)
        def _():
            ag_right(c, k).start()

        @pl.when(k > 0)
        def _():
            ag_left(c, k).start()

        cols = pl.ds(pl.multiple_of(c * CW, CW), CW)
        g_out[:, cols] = g
        new = BETA_TWO * second[:, cols] + (1.0 - BETA_TWO) * g * g
        direction = g / (jnp.sqrt(new) + GRAFT_EPS)
        d2[...] += jnp.sum((direction * direction).reshape(blk // 8, 8, CW), axis=0)

    def own_lag(j):
        return jnp.maximum(j, m - 1 - j)

    def gather_step(t):
        def near(d, _):
            below = k - d
            c_low = t - own_lag(below) - d

            @pl.when((below >= 0) & (c_low >= 0) & (c_low < nc))
            def _():
                ag_right(c_low, below).wait_recv()

                @pl.when(k < m - 1)
                def _():
                    ag_right(c_low, below).start()

            above = k + d
            c_high = t - own_lag(above) - d

            @pl.when((above < m) & (c_high >= 0) & (c_high < nc))
            def _():
                ag_left(c_high, above).wait_recv()

                @pl.when(k > 0)
                def _():
                    ag_left(c_high, above).start()

            return 0

        lax.fori_loop(1, m, near, 0)

    def times(lref, c):
        x = jnp.dot(lref[0], gbuf[c, pl.ds(0, win)], preferred_element_type=F32)
        for b in range(1, m):
            x += jnp.dot(lref[b], gbuf[c, pl.ds(b * win, win)], preferred_element_type=F32)
        return x

    def left_step(c):
        pps[c] = times(lr, c).astype(BF16)
        send_pp(c).start()

    def right_step(c):
        @pl.when(c == 0)
        def _():
            own_r.wait()

        x = times(lown, c)
        send_pp(c).wait_recv()
        x = (x + ppr[c].astype(F32)).astype(BF16)
        depth = pl.ds(pl.multiple_of(c * CW, CW), CW)

        def tile(j, _):
            cols = pl.ds(pl.multiple_of(j * 256, 256), 256)
            pre[:, cols] += jnp.dot(
                x, rv[depth, cols].astype(BF16), preferred_element_type=F32)
            return 0

        lax.fori_loop(0, pre.shape[1] // 256, tile, 0)

    first_lag = jnp.minimum(k, m - 1 - k)
    left_lag = m - 1 + own_lag(k)

    def at_lag(t, lag, f):
        @pl.when((t >= lag) & (t < nc + lag))
        def _():
            f(t - lag)

    def step(t, _):
        at_lag(t, first_lag, chunk_step)
        at_lag(t, k, right_pass)
        at_lag(t, m - 1 - k, left_pass)
        at_lag(t, own_lag(k), own_step)
        gather_step(t)

        @pl.when(t == 0)
        def _():
            cast_left()
            send_l.start()

        @pl.when(t == left_lag - 1)
        def _():
            send_l.wait_recv()
            fwd_l.start()

        @pl.when(t == left_lag)
        def _():
            got_l.wait_recv()

        at_lag(t, left_lag, left_step)
        at_lag(t, left_lag + 1, right_step)
        return 0

    lax.fori_loop(0, nc + left_lag + 1, step, 0)

    graft = jnp.sum(d2[...])
    x = pre[...]
    root = jnp.sum(x * x)
    rows8 = lax.broadcasted_iota(jnp.int32, (8, 128), 0)
    sv[me] = jnp.where(rows8 == 0, graft, root)

    def stat(peer, src):
        return remote(sv.at[src], sv.at[src], st_s.at[peer], st_r.at[src], rows=peer)

    def peer_of(i):
        return lax.rem(me + i, n)

    lax.fori_loop(1, n, lambda i, _: (stat(peer_of(i), me).start(), 0)[1], 0)

    def drain(c, _):
        send_c(c).wait_send()
        send_pp(c).wait_send()

        def each(b, _):
            @pl.when(c == 0)
            def _():
                send_at(b).wait_send()
                fwd_at(b).wait_send()

            @pl.when(b > k)
            def _():
                rs_right(c, b).wait_send()

            @pl.when(b < k)
            def _():
                rs_left(c, b).wait_send()

            @pl.when((b <= k) & (k < m - 1))
            def _():
                ag_right(c, b).wait_send()

            @pl.when((b >= k) & (k > 0))
            def _():
                ag_left(c, b).wait_send()

            return 0

        lax.fori_loop(0, m, each, 0)
        return 0

    lax.fori_loop(0, nc, drain, 0)
    send_l.wait_send()
    fwd_l.wait_send()
    lax.fori_loop(1, n, lambda i, _: (stat(peer_of(i), peer_of(i)).wait_recv(), 0)[1], 0)
    lax.fori_loop(1, n, lambda i, _: (stat(peer_of(i), me).wait_send(), 0)[1], 0)
    tot[...] = jnp.sum(sv[...], axis=0)


def per_device(n, wides, activations, cotangents, left_root, right_root, momentum, second_moment):
    tok, lb = activations.shape
    rb = cotangents.shape[1]
    blk = left_root.shape[0]
    m = n // 2
    nc = rb // CW
    win = -(-(blk + 128 - math.gcd(blk, 128)) // 128) * 128
    at_in = activations.T.reshape(m, 2, blk, tok)
    anywhere = pl.BlockSpec(memory_space=pl.ANY)
    vmem = pl.BlockSpec(memory_space=pltpu.VMEM)
    dma = pltpu.SemaphoreType.DMA
    pre, gradient, tot = pl.pallas_call(
        functools.partial(kernel, n, wides, m, nc, blk, tok, win),
        out_shape=(
            jax.ShapeDtypeStruct((blk, rb), F32),
            jax.ShapeDtypeStruct((blk, rb), F32),
            jax.ShapeDtypeStruct((8, 128), F32),
        ),
        in_specs=[anywhere, anywhere, anywhere, anywhere, vmem],
        out_specs=(vmem, vmem, vmem),
        scratch_shapes=[
            pltpu.VMEM((m, blk, 2 * tok), BF16),
            pltpu.VMEM((nc, 2 * tok, CW), BF16),
            pltpu.VMEM((nc, m, blk, CW), BF16),
            pltpu.VMEM((nc, m, blk, CW), BF16),
            pltpu.VMEM((nc, m * win, CW), BF16),
            pltpu.VMEM((blk, n * blk), F32),
            pltpu.VMEM((m, blk, win), BF16),
            pltpu.VMEM((m, blk, win), BF16),
            pltpu.VMEM((m, blk, win), BF16),
            pltpu.VMEM((nc, blk, CW), BF16),
            pltpu.VMEM((nc, blk, CW), BF16),
            pltpu.VMEM((rb, rb), F32),
            pltpu.VMEM((n, 8, 128), F32),
            pltpu.VMEM((8, CW), F32),
            dma((3,)), dma((nc,)), dma((2, m)), dma((2, m)), dma((nc,)), dma((nc,)),
            dma((2,)), dma((2,)),
            dma((nc, m)), dma((nc, m)), dma((nc, m)), dma((nc, m)),
            dma((nc, m)), dma((nc, m)), dma((nc, m)),
            dma((nc,)), dma((nc,)), dma((n,)), dma((n,)),
        ],
        compiler_params=pltpu.CompilerParams(
            collective_id=0, has_side_effects=True, vmem_limit_bytes=58 * 2**20,
        ),
    )(at_in, cotangents, left_root, right_root[0], second_moment)
    new_second = BETA_TWO * second_moment + (1.0 - BETA_TWO) * gradient * gradient
    factor = jnp.sqrt(tot[0, 0]) / jnp.sqrt(tot[1, 0] + NORM_EPS)
    new_momentum = BETA_ONE * momentum + factor * pre
    return (new_momentum, new_second)


def solution(mesh):
    placed = (
        P(("groups", "rows"), None),
        P(("groups", "rows"), "wide"),
        P(("groups", "rows"), None),
        P(("groups", "wide"), None, None),
        P(("groups", "rows"), "wide"),
        P(("groups", "rows"), "wide"),
    )
    return jax.shard_map(
        functools.partial(per_device, mesh.shape["rows"], mesh.shape["wide"]),
        mesh=mesh,
        in_specs=placed,
        out_specs=(P(("groups", "rows"), "wide"), P(("groups", "rows"), "wide")),
        check_vma=False,
    )
```

```python
import functools
import math

import jax
import jax.numpy as jnp
from jax import lax
from jax.experimental import pallas as pl
from jax.experimental.pallas import tpu as pltpu
from jax.sharding import PartitionSpec as P

BETA_ONE = 0.9
BETA_TWO = 0.99
GRAFT_EPS = 1e-08
NORM_EPS = 1e-06
CW = 128
MESH = pl.DeviceIdType.MESH
F32 = jnp.float32
BF16 = jnp.bfloat16


def kernel(
    n, wides, m, nc, blk, tok, win,
    at_in, c_in, l_in, r_in, second,
    pre, g_out, tot,
    at2, cc, rbuf, lbuf, gbuf, lf, lown, ls, lr, pps, ppr, rv, sv, d2,
    loc, locc, xa_s, xa_r, xc_s, xc_r, xl_s, xl_r,
    rr_s, rr_r, rl_s, rl_r, ga_r, gr_s, gl_s, pp_s, pp_r, st_s, st_r,
):
    me = lax.axis_index("rows")
    w = lax.axis_index("wide")
    k = me // 2
    p = me % 2
    other = 1 - w
    partner = k * 2 + (1 - p)
    right = jnp.minimum(k + 1, m - 1) * 2 + p
    left = jnp.maximum(k - 1, 0) * 2 + p
    mh = m // wides

    def remote(src, dst, ss, rs, **to):
        return pltpu.make_async_remote_copy(
            src_ref=src, dst_ref=dst, send_sem=ss, recv_sem=rs,
            device_id=to, device_id_type=MESH,
        )

    own_at = pltpu.make_async_copy(at_in.at[:, p], at2.at[:, :, pl.ds(0, tok)], loc.at[0])
    own_l = pltpu.make_async_copy(l_in, lf, loc.at[1])
    own_r = pltpu.make_async_copy(r_in, rv, loc.at[2])

    def own_c(c):
        cols = pl.ds(pl.multiple_of(c * CW, CW), CW)
        return pltpu.make_async_copy(c_in.at[:, cols], cc.at[c, pl.ds(0, tok)], locc.at[c])

    half = pl.ds(w * mh, mh)
    ohalf = pl.ds(other * mh, mh)
    part = pl.ds(tok, tok)
    tw = tok // wides
    part_w = pl.ds(pl.multiple_of(tok + w * tw, tw), tw)
    part_o = pl.ds(pl.multiple_of(tok + other * tw, tw), tw)
    token_w = pl.ds(pl.multiple_of(w * tw, tw), tw)

    def send_at(b):
        return remote(
            at_in.at[b, 1 - p, :, token_w], at2.at[b, :, part_w], xa_s.at[0, b], xa_r.at[0, b],
            rows=partner)

    def fwd_at(b):
        return remote(
            at2.at[b, :, part_w], at2.at[b, :, part_w], xa_s.at[1, b], xa_r.at[1, b], wide=other)

    def got_at(b):
        return remote(
            at2.at[b, :, part_o], at2.at[b, :, part_o], xa_s.at[1, b], xa_r.at[1, b], wide=other)

    def far_first(f):
        def both(i, _):
            d = m - 1 - i

            @pl.when(k + d < m)
            def _():
                f(k + d)

            @pl.when(k - d >= 0)
            def _():
                f(k - d)

            return 0

        lax.fori_loop(0, m - 1, both, 0)
        f(k)

    def window(b, q):
        first = (2 * b + q) * blk
        start = jnp.minimum(first // 128 * 128, n * blk - win)
        return pl.multiple_of(start, 128), first - start

    send_l = remote(ls.at[half], lr.at[half], xl_s.at[0], xl_r.at[0], rows=partner)
    fwd_l = remote(lr.at[half], lr.at[half], xl_s.at[1], xl_r.at[1], wide=other)
    got_l = remote(lr.at[ohalf], lr.at[ohalf], xl_s.at[1], xl_r.at[1], wide=other)

    def send_c(c):
        cols = pl.ds(pl.multiple_of(c * CW, CW), CW)
        return remote(
            c_in.at[:, cols], cc.at[c, part], xc_s.at[c], xc_r.at[c], rows=partner)

    def rs_right(c, b):
        return remote(
            rbuf.at[c, b], rbuf.at[c, b], rr_s.at[c, b], rr_r.at[c, b], rows=right)

    def rs_left(c, b):
        return remote(lbuf.at[c, b], lbuf.at[c, b], rl_s.at[c, b], rl_r.at[c, b], rows=left)

    def block_rows(b):
        return pl.ds(pl.multiple_of(b * win + window(b, p)[1], 16), blk)

    def ag_right(c, b):
        ref = gbuf.at[c, block_rows(b)]
        return remote(ref, ref, gr_s.at[c, b], ga_r.at[c, b], rows=right)

    def ag_left(c, b):
        ref = gbuf.at[c, block_rows(b)]
        return remote(ref, ref, gl_s.at[c, b], ga_r.at[c, b], rows=left)

    def send_pp(c):
        return remote(pps.at[c], ppr.at[c], pp_s.at[c], pp_r.at[c], rows=partner)

    barrier = pltpu.get_barrier_semaphore()

    def greet(i, _):
        pl.semaphore_signal(
            barrier, inc=1, device_id={"rows": lax.rem(me + i, n)}, device_id_type=MESH)
        return 0

    own_at.start()
    lax.fori_loop(0, nc, lambda c, _: (own_c(c).start(), 0)[1], 0)
    lax.fori_loop(1, n, greet, 0)
    pl.semaphore_signal(barrier, inc=1, device_id={"wide": other}, device_id_type=MESH)
    gbuf[...] = jnp.zeros_like(gbuf)

    @pl.when(k == 0)
    def _():
        rbuf[...] = jnp.zeros_like(rbuf)

    @pl.when(k == m - 1)
    def _():
        lbuf[...] = jnp.zeros_like(lbuf)

    pl.semaphore_wait(barrier, n)

    send_c(0).start()
    far_first(lambda b: send_at(b).start())
    for ahead in range(1, min(4, nc)):
        send_c(ahead).start()
    own_l.start()
    own_r.start()
    d2[...] = jnp.zeros_like(d2)
    pre[...] = jnp.zeros_like(pre)
    own_at.wait()

    def arrive(c, b):
        @pl.when(c == 0)
        def _():
            send_at(b).wait_recv()
            fwd_at(b).start()
            got_at(b).wait_recv()

    def cast_left():
        own_l.wait()

        def one(b, _):
            mine, _ = window(b, p)
            theirs, _ = window(b, 1 - p)
            ls[b] = lf[:, pl.ds(theirs, win)].astype(BF16)
            lown[b] = lf[:, pl.ds(mine, win)].astype(BF16)
            return 0

        lax.fori_loop(0, m, one, 0)

    def term(c, b):
        return jnp.dot(at2[b], cc[c], preferred_element_type=F32)

    def chunk_step(c):
        @pl.when(c + 4 < nc)
        def _():
            send_c(c + 4).start()

        own_c(c).wait()
        send_c(c).wait_recv()

    def right_pass(c):
        def one(i, _):
            b = m - 1 - i
            arrive(c, b)
            x = term(c, b)

            @pl.when(k > 0)
            def _():
                rs_right(c, b).wait_recv()

            rbuf[c, b] = (x + rbuf[c, b].astype(F32)).astype(BF16)
            rs_right(c, b).start()
            return 0

        lax.fori_loop(0, m - 1 - k, one, 0)

    def left_pass(c):
        def one(b, _):
            arrive(c, b)
            x = term(c, b)

            @pl.when(k < m - 1)
            def _():
                rs_left(c, b).wait_recv()

            lbuf[c, b] = (x + lbuf[c, b].astype(F32)).astype(BF16)
            rs_left(c, b).start()
            return 0

        lax.fori_loop(0, k, one, 0)

    def own_step(c):
        arrive(c, k)
        x = term(c, k)

        @pl.when(k > 0)
        def _():
            rs_right(c, k).wait_recv()

        @pl.when(k < m - 1)
        def _():
            rs_left(c, k).wait_recv()

        g = x + rbuf[c, k].astype(F32) + lbuf[c, k].astype(F32)
        gbuf[c, block_rows(k)] = g.astype(BF16)

        @pl.when(k < m - 1)
        def _():
            ag_right(c, k).start()

        @pl.when(k > 0)
        def _():
            ag_left(c, k).start()

        cols = pl.ds(pl.multiple_of(c * CW, CW), CW)
        g_out[:, cols] = g
        new = BETA_TWO * second[:, cols] + (1.0 - BETA_TWO) * g * g
        direction = g / (jnp.sqrt(new) + GRAFT_EPS)
        d2[...] += jnp.sum((direction * direction).reshape(blk // 8, 8, CW), axis=0)

    def own_lag(j):
        return jnp.maximum(j, m - 1 - j)

    def gather_step(t):
        def near(d, _):
            below = k - d
            c_low = t - own_lag(below) - d

            @pl.when((below >= 0) & (c_low >= 0) & (c_low < nc))
            def _():
                ag_right(c_low, below).wait_recv()

                @pl.when(k < m - 1)
                def _():
                    ag_right(c_low, below).start()

            above = k + d
            c_high = t - own_lag(above) - d

            @pl.when((above < m) & (c_high >= 0) & (c_high < nc))
            def _():
                ag_left(c_high, above).wait_recv()

                @pl.when(k > 0)
                def _():
                    ag_left(c_high, above).start()

            return 0

        lax.fori_loop(1, m, near, 0)

    def times(lref, c):
        x = jnp.dot(lref[0], gbuf[c, pl.ds(0, win)], preferred_element_type=F32)
        for b in range(1, m):
            x += jnp.dot(lref[b], gbuf[c, pl.ds(b * win, win)], preferred_element_type=F32)
        return x

    def left_step(c):
        pps[c] = times(lr, c).astype(BF16)
        send_pp(c).start()

    def right_step(c):
        @pl.when(c == 0)
        def _():
            own_r.wait()

        x = times(lown, c)
        send_pp(c).wait_recv()
        x = (x + ppr[c].astype(F32)).astype(BF16)
        depth = pl.ds(pl.multiple_of(c * CW, CW), CW)

        def tile(j, _):
            cols = pl.ds(pl.multiple_of(j * 256, 256), 256)
            pre[:, cols] += jnp.dot(
                x, rv[depth, cols].astype(BF16), preferred_element_type=F32)
            return 0

        lax.fori_loop(0, pre.shape[1] // 256, tile, 0)

    first_lag = jnp.minimum(k, m - 1 - k)
    left_lag = m - 1 + own_lag(k)

    def at_lag(t, lag, f):
        @pl.when((t >= lag) & (t < nc + lag))
        def _():
            f(t - lag)

    def step(t, _):
        at_lag(t, first_lag, chunk_step)
        at_lag(t, k, right_pass)
        at_lag(t, m - 1 - k, left_pass)
        at_lag(t, own_lag(k), own_step)
        gather_step(t)

        @pl.when(t == 1)
        def _():
            cast_left()
            send_l.start()

        @pl.when(t == left_lag - 1)
        def _():
            send_l.wait_recv()
            fwd_l.start()

        @pl.when(t == left_lag)
        def _():
            got_l.wait_recv()

        at_lag(t, left_lag, left_step)
        at_lag(t, left_lag + 1, right_step)
        return 0

    lax.fori_loop(0, nc + left_lag + 1, step, 0)

    graft = jnp.sum(d2[...])
    x = pre[...]
    root = jnp.sum(x * x)
    rows8 = lax.broadcasted_iota(jnp.int32, (8, 128), 0)
    sv[me] = jnp.where(rows8 == 0, graft, root)

    def stat(peer, src):
        return remote(sv.at[src], sv.at[src], st_s.at[peer], st_r.at[src], rows=peer)

    def peer_of(i):
        return lax.rem(me + i, n)

    lax.fori_loop(1, n, lambda i, _: (stat(peer_of(i), me).start(), 0)[1], 0)

    def drain(c, _):
        send_c(c).wait_send()
        send_pp(c).wait_send()

        def each(b, _):
            @pl.when(c == 0)
            def _():
                send_at(b).wait_send()
                fwd_at(b).wait_send()

            @pl.when(b > k)
            def _():
                rs_right(c, b).wait_send()

            @pl.when(b < k)
            def _():
                rs_left(c, b).wait_send()

            @pl.when((b <= k) & (k < m - 1))
            def _():
                ag_right(c, b).wait_send()

            @pl.when((b >= k) & (k > 0))
            def _():
                ag_left(c, b).wait_send()

            return 0

        lax.fori_loop(0, m, each, 0)
        return 0

    lax.fori_loop(0, nc, drain, 0)
    send_l.wait_send()
    fwd_l.wait_send()
    lax.fori_loop(1, n, lambda i, _: (stat(peer_of(i), peer_of(i)).wait_recv(), 0)[1], 0)
    lax.fori_loop(1, n, lambda i, _: (stat(peer_of(i), me).wait_send(), 0)[1], 0)
    tot[...] = jnp.sum(sv[...], axis=0)


def per_device(n, wides, activations, cotangents, left_root, right_root, momentum, second_moment):
    tok, lb = activations.shape
    rb = cotangents.shape[1]
    blk = left_root.shape[0]
    m = n // 2
    nc = rb // CW
    win = -(-(blk + 128 - math.gcd(blk, 128)) // 128) * 128
    at_in = activations.T.reshape(m, 2, blk, tok)
    anywhere = pl.BlockSpec(memory_space=pl.ANY)
    vmem = pl.BlockSpec(memory_space=pltpu.VMEM)
    dma = pltpu.SemaphoreType.DMA
    pre, gradient, tot = pl.pallas_call(
        functools.partial(kernel, n, wides, m, nc, blk, tok, win),
        out_shape=(
            jax.ShapeDtypeStruct((blk, rb), F32),
            jax.ShapeDtypeStruct((blk, rb), F32),
            jax.ShapeDtypeStruct((8, 128), F32),
        ),
        in_specs=[anywhere, anywhere, anywhere, anywhere, vmem],
        out_specs=(vmem, vmem, vmem),
        scratch_shapes=[
            pltpu.VMEM((m, blk, 2 * tok), BF16),
            pltpu.VMEM((nc, 2 * tok, CW), BF16),
            pltpu.VMEM((nc, m, blk, CW), BF16),
            pltpu.VMEM((nc, m, blk, CW), BF16),
            pltpu.VMEM((nc, m * win, CW), BF16),
            pltpu.VMEM((blk, n * blk), F32),
            pltpu.VMEM((m, blk, win), BF16),
            pltpu.VMEM((m, blk, win), BF16),
            pltpu.VMEM((m, blk, win), BF16),
            pltpu.VMEM((nc, blk, CW), BF16),
            pltpu.VMEM((nc, blk, CW), BF16),
            pltpu.VMEM((rb, rb), F32),
            pltpu.VMEM((n, 8, 128), F32),
            pltpu.VMEM((8, CW), F32),
            dma((3,)), dma((nc,)), dma((2, m)), dma((2, m)), dma((nc,)), dma((nc,)),
            dma((2,)), dma((2,)),
            dma((nc, m)), dma((nc, m)), dma((nc, m)), dma((nc, m)),
            dma((nc, m)), dma((nc, m)), dma((nc, m)),
            dma((nc,)), dma((nc,)), dma((n,)), dma((n,)),
        ],
        compiler_params=pltpu.CompilerParams(
            collective_id=0, has_side_effects=True, vmem_limit_bytes=58 * 2**20,
        ),
    )(at_in, cotangents, left_root, right_root[0], second_moment)
    new_second = BETA_TWO * second_moment + (1.0 - BETA_TWO) * gradient * gradient
    factor = jnp.sqrt(tot[0, 0]) / jnp.sqrt(tot[1, 0] + NORM_EPS)
    new_momentum = BETA_ONE * momentum + factor * pre
    return (new_momentum, new_second)


def solution(mesh):
    placed = (
        P(("groups", "rows"), None),
        P(("groups", "rows"), "wide"),
        P(("groups", "rows"), None),
        P(("groups", "wide"), None, None),
        P(("groups", "rows"), "wide"),
        P(("groups", "rows"), "wide"),
    )
    return jax.shard_map(
        functools.partial(per_device, mesh.shape["rows"], mesh.shape["wide"]),
        mesh=mesh,
        in_specs=placed,
        out_specs=(P(("groups", "rows"), "wide"), P(("groups", "rows"), "wide")),
        check_vma=False,
    )
```
